128 devices in a mesh: gx: 32 (over z, x, core), gy: 4 (over y).
Axes of the slice: x: 4, y: 4, z: 4, core: 2. Of those that a mesh axis runs over, the one named last changes fastest.
Arguments:
- state: float32 [4, 1024, 512, 128], P(None, 'gx', 'gy'), may hold values from -6 to 6
- velocity: float32 [3, 1024, 512, 128], P(None, 'gx', 'gy'), may hold values from -6 to 6
- threshold: float32 [32, 512], P('gx', 'gy'), may hold values from 0.5 to 3
- tile_owner: int32 [4, 1024, 1], P('gy', 'gx'), may hold values from 0 to 31; in each aligned block of 32 rows (0 to 31, 32 to 63, ..., all dimensions but the last counted through in order) at most 2 rows name the same one
- parcel_owner: int32 [4, 1024, 1], P('gy', 'gx'), may hold values from 0 to 31; in each aligned block of 32 rows (0 to 31, 32 to 63, ..., all dimensions but the last counted through in order) at most 2 rows name the same one
- parcel_count: int32 [4, 1024], P('gy', 'gx'), may hold values from 1 to 128, as said below
- parcel_share: float32 [4, 1024, 128], P('gy', 'gx'), may hold values from 0.2 to 1
Outputs:
- fields: float32 [4, 1024, 512, 128], P(None, 'gx', 'gy')
- ground_flux: float32 [32, 512], P('gx', 'gy')
The draws below stay inside these ranges and needn't reach their ends.
Inputs may be any that keep to these rules, and one draw needn't show every extreme that they name: `tile_owner`: among the 32 tiles of one device no owner is named more than 2 times, and that count is reached. `parcel_owner`: among the 32 rows of one owner no destination is named more than 2 times, and that count is reached. `parcel_count`: the first row of every owner has 128 live parcels.
All inputs are finite; a program needn't handle non-finite values.
Results may differ from the reference program's by a relative error of at most 0.0003.
Values sent between devices are 32-bit elements; how exact they have to be, the bound alone decides.
A program may use at most 256 MiB of HBM per device.

```python
import math
import jax
import jax.numpy as jnp
import numpy as np
from jax import lax

CX = 32
CY = 128
LEVELS = 4
ROWS_DEV = 32
STEPS = 2
CAP = 2
RCAP = 2
NX = 1024
NY = 512
NZ = 128
ROWS = 1024
N_GX = 32
N_GY = 4


def draw_parcel_count(key, part):
    values = jax.random.randint(key, (N_GY, ROWS), 1, CY + 1)
    column = jnp.arange(ROWS)[None, :] % ROWS_DEV
    return jnp.where(column == 0, CY, values).astype(jnp.int32)


def block_levels(stream_key, dims, shards, low, top_value):
    def one(axis_at, parts):
        steps = jax.random.uniform(jax.random.fold_in(jax.random.fold_in(stream_key, 6), axis_at), (parts,), jnp.float32, low / len(shards), top_value / len(shards))
        return jnp.repeat(jnp.exp(steps), dims[axis_at] // parts).reshape((-1,) + (1,) * (len(dims) - axis_at - 1))

    level = one(*shards[0])
    for cut in shards[1:]:
        level = level * one(*cut)
    return level


def shared_out(stream_key, own, number, rows, count, top, bound, lean):
    order = jax.random.permutation(stream_key, count)
    heavy_load, usual = portions_of(count, rows * top, bound, lean, True), portions_of(count, rows * top, bound, lean, False)
    places = jnp.arange(count)

    def named(lengths, turn):
        used = int((lengths > 0).sum())
        fixed = max(1, used // 4)
        moved = fixed + (places - fixed + turn * (used - fixed)) % max(1, count - fixed)
        return jnp.zeros((count,), jnp.int32).at[order[jnp.where(places < fixed, places, moved)]].set(jnp.asarray(lengths, jnp.int32))

    lengths = jnp.where(number % 4 == 0, named(heavy_load, number // 4), named(usual, number - number // 4 - 1))
    mixed = jax.random.permutation(jax.random.fold_in(own, 3), count)
    donor, receiver = mixed[0:count // 2 * 2:2], mixed[1:count // 2 * 2:2]
    margin = jnp.minimum(lengths[donor] - 1, bound - lengths[receiver]) // 2
    margin = jnp.where((donor == order[0]) | (receiver == order[0]) | (lengths[receiver] == 0), 0, jnp.maximum(margin, 0))
    moved = jax.random.randint(jax.random.fold_in(own, 4), (count // 2,), 0, 1 << 20) % (margin + 1)
    lengths = lengths.at[donor].add(-moved).at[receiver].add(moved)
    labels = jnp.searchsorted(jnp.cumsum(lengths), jnp.arange(rows * top), side="right").astype(jnp.int32)
    grid = labels.reshape(top, rows).T
    grid = grid[jax.random.permutation(jax.random.fold_in(own, 1), rows)]
    turn = jax.random.randint(jax.random.fold_in(own, 2), (rows, 1), 0, top)
    return jnp.take_along_axis(grid, (jnp.arange(top)[None, :] + turn) % top, axis=1)


def portions_of(number_of, total, most, slope, full):
    loads = [(1 << 20) // math.isqrt(standing ** slope) + 1 for standing in range(1, number_of + 1)]
    largest = most if full else min(most, max(-(-total // number_of), total * loads[0] // sum(loads)))
    least = 1 if total - largest >= number_of - 1 else 0
    given, rest = [largest] + [least] * (number_of - 1), total - largest - least * (number_of - 1)
    while rest > 0:
        movable = [i for i in range(1, number_of) if given[i] < largest] or [i for i in range(1, number_of) if given[i] < most]
        whole, budget = sum([loads[i] for i in movable]), rest
        for i in movable:
            addition = min(most - given[i], max(1, budget * loads[i] // whole), rest)
            given[i] = given[i] + addition
            rest = rest - addition
    return np.array(given)


def noise(rng, dims, scale, most, pieces=(), dtype=jnp.bfloat16):
    result = scale * jax.random.normal(rng, dims, jnp.float32)
    if pieces:
        result = result * block_levels(rng, dims, pieces, -0.22, 0.18)
    return jnp.clip(result, -most, most).astype(dtype)


def setup_inputs(seed: int = 0) -> dict:
    seeds = jax.random.split(jax.random.key(seed), 8)
    state = noise(seeds[0], (4, NX, NY, NZ), 1.0, 6.0, ((1, 32), (2, 4)), jnp.float32)
    velocity = noise(seeds[1], (3, NX, NY, NZ), 1.0, 6.0, ((1, 32), (2, 4)), jnp.float32)
    threshold = jnp.clip(jnp.exp(math.log(3.0) - 1.7917595 * jax.random.uniform(seeds[2], (N_GX, NY), jnp.float32) ** block_levels(seeds[2], (N_GX, NY), ((0, 32), (1, 4)), -0.2, 0.2)), 0.5, 3.0)
    tile_owner_keys = jax.random.split(jax.random.fold_in(seeds[3], 1), N_GY * NX // CX)
    tile_owner_turns = jax.random.permutation(jax.random.fold_in(seeds[3], 3), N_GY * NX // CX)
    tile_owner = jax.vmap(lambda own, number: shared_out(jax.random.fold_in(seeds[3], 2), own, number, CX, N_GX, 1, CAP, 2))(tile_owner_keys, tile_owner_turns).reshape((N_GY, NX, 1))
    parcel_owner_keys = jax.random.split(jax.random.fold_in(seeds[4], 1), N_GY * ROWS // ROWS_DEV)
    parcel_owner_turns = jax.random.permutation(jax.random.fold_in(seeds[4], 3), N_GY * ROWS // ROWS_DEV)
    parcel_owner = jax.vmap(lambda own, number: shared_out(jax.random.fold_in(seeds[4], 2), own, number, ROWS_DEV, N_GX, 1, RCAP, 2))(parcel_owner_keys, parcel_owner_turns).reshape((N_GY, ROWS, 1))
    parcel_count = draw_parcel_count(jax.random.fold_in(seeds[7], 71), 0)
    parcel_share = jnp.clip(0.2 + 0.8 * jax.random.uniform(seeds[6], (N_GY, ROWS, CY), jnp.float32) ** block_levels(seeds[6], (N_GY, ROWS, CY), ((0, 4), (1, 32)), -0.2, 0.2), 0.2, 1.0)
    return {"state": state, "velocity": velocity, "threshold": threshold, "tile_owner": tile_owner, "parcel_owner": parcel_owner, "parcel_count": parcel_count, "parcel_share": parcel_share}


profile_weights = (0.4, 0.3, 0.2, 0.1)
time_step = 0.1


def friction(east, north):
    total = profile_weights[0] * (east[..., 0, :] * east[..., 0, :] + north[..., 0, :] * north[..., 0, :])
    for level in range(1, east.shape[-2]):
        total = total + profile_weights[level] * (east[..., level, :] * east[..., level, :] + north[..., level, :] * north[..., level, :])
    return total


def minmod(first, second):
    return jnp.where(first * second > 0, jnp.sign(first) * jnp.minimum(jnp.abs(first), jnp.abs(second)), 0.0)


def section(array, axis, start, stop):
    return lax.slice_in_dim(array, start, stop, axis=axis)


def divergence(field, speed, axis):
    count = field.shape[axis] - 4
    behind = section(field, axis, 0, count + 1)
    here = section(field, axis, 1, count + 2)
    ahead = section(field, axis, 2, count + 3)
    beyond = section(field, axis, 3, count + 4)
    face_speed = 0.5 * (section(speed, axis, 1, count + 2) + section(speed, axis, 2, count + 3))
    upwind = face_speed * (here + 0.5 * minmod(ahead - here, here - behind))
    downwind = face_speed * (ahead - 0.5 * minmod(beyond - ahead, ahead - here))
    fluxes = jnp.where(face_speed > 0, upwind, downwind)
    return section(fluxes, axis, 1, count + 1) - section(fluxes, axis, 0, count)


def advance(padded, wind):
    inner = padded[:, 2:-2, 2:-2, 2:-2]
    along_x = divergence(padded[:, :, 2:-2, 2:-2], wind[0:1, :, 2:-2, 2:-2], 1)
    along_y = divergence(padded[:, 2:-2, :, 2:-2], wind[1:2, 2:-2, :, 2:-2], 2)
    along_z = divergence(padded[:, 2:-2, 2:-2, :], wind[2:3, 2:-2, 2:-2, :], 3)
    return inner - time_step * (along_x + along_y + along_z)


def reference(state, velocity, threshold, tile_owner, parcel_owner, parcel_count, parcel_share):
    highest = lax.Precision.HIGHEST
    east = velocity[0, :, :, 0:LEVELS].reshape(NX, N_GY, CY, LEVELS).transpose(1, 0, 3, 2)
    north = velocity[1, :, :, 0:LEVELS].reshape(NX, N_GY, CY, LEVELS).transpose(1, 0, 3, 2)
    stress = friction(east, north)
    owners = tile_owner[:, :, 0]
    choose = (owners[:, :, None] == jnp.arange(N_GX)[None, None, :]).astype(jnp.float32)
    limits = threshold.reshape(N_GX, N_GY, CY).transpose(1, 0, 2)
    tile_limit = jnp.einsum("yxo,yoj->yxj", choose, limits, precision=highest)
    lifting = jnp.maximum(stress - tile_limit, 0.0)
    patch = jnp.einsum("yxo,yxj->yoj", choose, lifting, precision=highest) / CX
    ground_flux = patch.transpose(1, 0, 2).reshape(N_GX, NY)
    source = jnp.arange(ROWS) // ROWS_DEV
    row_flux = patch[:, source, :]
    reach = (jnp.arange(CY)[None, None, :] < parcel_count[:, :, None]).astype(jnp.float32)
    masses = row_flux * parcel_share * reach
    landing_x = parcel_owner[:, :, 0] * CX + source[None, :] % CX
    place = (landing_x[:, :, None] == jnp.arange(NX)[None, None, :]).astype(jnp.float32)
    deposit = jnp.einsum("yrx,yrj->yxj", place, masses, precision=highest)
    deposit = deposit.transpose(1, 0, 2).reshape(NX, NY)
    fields = state.at[3, :, :, 0].add(deposit)
    wind = jnp.pad(velocity, ((0, 0), (2, 2), (2, 2), (2, 2)))
    for substep in range(STEPS):
        fields = lax.map(lambda component: advance(jnp.pad(component, 2)[None], wind)[0], fields)
    return fields, ground_flux
```

```python
import functools

import jax
import jax.numpy as jnp
from jax import lax
from jax.experimental import pallas as pl
from jax.experimental.pallas import tpu as pltpu
from jax.sharding import PartitionSpec as P

MESH = pl.DeviceIdType.MESH
f32 = jnp.float32
profile_weights = (0.4, 0.3, 0.2, 0.1)
SCALE = 0.1 * 0.25
X = 32
PAIRS = X // 2
ROWS = 144
OWN = pl.ds(8, 128)
N = 17
GX, GY = 32, 4


def S(k):
    return pl.ds(4 + k, 8, stride=N)


def A(k):
    return pl.ds(8 * k, 8)


def minmod(a, b):
    return jnp.maximum(jnp.minimum(a, b), jnp.minimum(jnp.maximum(a, b), 0.0))


def rollup(v):
    return pltpu.roll(v, 7, 0)


def rolldn(v):
    return pltpu.roll(v, 1, 0)


class Line:
    def __init__(self, load):
        self.load = load
        v0, v15, v16 = load(0), load(15), load(16)
        wrap = rollup(v0) - v16
        before = v16 - v15
        twice = v16 + v16
        m = minmod(wrap, before)
        self.tail = (twice + m, twice - m, before)
        self.v = v0
        self.d = rolldn(wrap)
        self.l = rolldn(twice + m)
        self.f = None

    def step(self, k, w, mask):
        if k == 16:
            l, r, d = self.tail
        else:
            v = self.v
            ahead = self.load(k + 1)
            d = ahead - v if k < 15 else self.tail[2]
            if k % 2 == 0:
                self.clip = jnp.maximum(d, 0.0), jnp.minimum(d, 0.0)
                m = jnp.maximum(jnp.minimum(self.d, self.clip[0]), self.clip[1])
            else:
                m = jnp.maximum(jnp.minimum(d, self.clip[0]), self.clip[1])
            twice = v + v
            l, r = twice + m, twice - m
            self.v = ahead
        f = w * jnp.where(mask, self.l, r)
        out = None if self.f is None else f - self.f
        if k == 0:
            self.first = rollup(f)
        self.f, self.l, self.d = f, l, d
        return out

    def end(self):
        return self.first - self.f


def turn_in(i, c, b, q, qt):
    qt[2 * c + b, OWN, :] = q[c, i + 2 + b, OWN, :].T


def turn_out(c, b, zt, az):
    az[2 * c + b, OWN, :] = zt[2 * c + b, OWN, :].T


def zplane(i, b, comps, qt, zt, wz):
    lines = {c: Line(lambda k, c=c: qt[2 * c + b, S(k), :]) for c in comps}
    for k in range(N):
        w = wz[i + b, A(k), :]
        mask = w > 0
        for c in comps:
            out = lines[c].step(k, w, mask)
            if k:
                zt[2 * c + b, S(k - 1), :] = out
    for c in comps:
        zt[2 * c + b, S(16), :] = lines[c].end()


def xypair(i, comps, q, write, wx, wy, az, cx):
    lines = {
        (c, b): Line(lambda k, c=c, b=b: q[c, i + 2 + b, S(k), :]) for c in comps for b in range(2)
    }
    for k in range(N + 1):
        acc = {}
        if k < N:
            for b in range(2):
                w = wy[i + b, A(k), :]
                mask = w > 0
                for c in comps:
                    acc[c, b] = lines[c, b].step(k, w, mask)
        else:
            for key, line in lines.items():
                acc[key] = line.end()
        if k == 0:
            continue
        u = k - 1
        w0 = wx[i + 1, A(u), :]
        w1 = wx[i + 2, A(u), :]
        m0, m1 = w0 > 0, w1 > 0
        for c in comps:
            q1 = q[c, i + 3, S(u), :]
            q2 = q[c, i + 4, S(u), :]
            db = q2 - q1
            dc = q[c, i + 5, S(u), :] - q2
            high, low = jnp.maximum(db, 0.0), jnp.minimum(db, 0.0)
            s1 = jnp.maximum(jnp.minimum(cx[c, 0, A(u), :], high), low)
            s2 = jnp.maximum(jnp.minimum(dc, high), low)
            t1 = q1 + q1
            t2 = q2 + q2
            f0 = w0 * jnp.where(m0, cx[c, 1, A(u), :], t1 - s1)
            f1 = w1 * jnp.where(m1, t1 + s1, t2 - s2)
            fm = cx[c, 2, A(u), :]
            cx[c, 0, A(u), :] = dc
            cx[c, 1, A(u), :] = t2 + s2
            cx[c, 2, A(u), :] = f1
            write(c, i, u, q[c, i + 2, S(u), :] - ((f0 - fm) + (acc[c, 0] + az[2 * c, S(u), :])))
            write(c, i + 1, u, q1 - ((f1 - f0) + (acc[c, 1] + az[2 * c + 1, S(u), :])))


def xstart(comps, q, wx, cx):
    for u in range(N):
        w = wx[0, A(u), :]
        mask = w > 0
        for c in comps:
            qa, qb, qc, qd = (q[c, p, S(u), :] for p in range(4))
            db, dc = qc - qb, qd - qc
            left = (qb + qb) + minmod(qb - qa, db)
            m = minmod(db, dc)
            twice = qc + qc
            cx[c, 0, A(u), :] = dc
            cx[c, 1, A(u), :] = twice + m
            cx[c, 2, A(u), :] = w * jnp.where(mask, left, twice - m)


def zstart(groups, q, qt, zt, wz):
    for comps in groups:
        for b in range(2):
            for c in comps:
                turn_in(0, c, b, q, qt)
    for comps in groups:
        for b in range(2):
            zplane(0, b, comps, qt, zt, wz)
            for c in comps:
                turn_in(2, c, b, q, qt)


def sweep_step(j, groups, q, write, wx, wy, wz, cx, qt, zt, az):
    i = 2 * j
    nxt = jnp.minimum(i + 2, X - 2)
    nxt2 = jnp.minimum(i + 4, X - 2)
    for comps in groups:
        for b in range(2):
            for c in comps:
                turn_out(c, b, zt, az)
    for comps in groups:
        for b in range(2):
            zplane(nxt, b, comps, qt, zt, wz)
            for c in comps:
                turn_in(nxt2, c, b, q, qt)
    for comps in groups:
        xypair(i, comps, q, write, wx, wy, az, cx)


def clear_turned(qt):
    zero = jnp.zeros((8, 128), f32)
    for s in range(8):
        qt[s, 0:8, :] = zero
        qt[s, 136:144, :] = zero


def first_kernel(
    state, vel, thr, tile, parcel, count, share,
    q1, wxo, wyo, wzo, flux_out,
    q, v, q1v, wx, wy, wz, cx, qt, zt, az, stress, packed, got, rows, landed, zeros, zrows,
    load_sem, lsend, lrecv, a2a_sem, out_sem,
):
    gx, gy = lax.axis_index("gx"), lax.axis_index("gy")

    def local(src, dst, s):
        return pltpu.make_async_copy(src, dst, load_sem.at[s])

    loads = [
        local(vel.at[a], v.at[a, pl.ds(1, X), OWN, :], a) for a in range(3)
    ] + [local(state.at[c], q.at[c, pl.ds(2, X), OWN, :], 3 + c) for c in range(4)]
    for copy in loads:
        copy.start()

    target = (gx < GX - 1, gx > 0, gy < GY - 1, gy > 0)
    source = (gx > 0, gx < GX - 1, gy > 0, gy < GY - 1)
    where = (
        {"gx": lax.rem(gx + 1, GX)},
        {"gx": lax.rem(gx + GX - 1, GX)},
        {"gy": lax.rem(gy + 1, GY)},
        {"gy": lax.rem(gy + GY - 1, GY)},
    )

    class Exchange:
        def __init__(self, g, pieces):
            self.copies = [
                pltpu.make_async_remote_copy(
                    src_ref=src, dst_ref=dst, send_sem=lsend.at[g, n], recv_sem=lrecv.at[g, n],
                    device_id=where[n], device_id_type=MESH,
                )
                for n, (src, dst) in enumerate(pieces)
            ]

        def each(self, flags, act):
            for flag, copy in zip(flags, self.copies):
                @pl.when(flag)
                def _(copy=copy):
                    act(copy)

        def start(self):
            self.each(target, lambda copy: copy.start())

        def wait_recv(self):
            self.each(source, lambda copy: copy.wait_recv())

        def wait_send(self):
            self.each(target, lambda copy: copy.wait_send())

    all_x = pl.ds(2, X)
    wind = Exchange(0, [
        (vel.at[0, X - 1], v.at[0, 0, OWN, :]),
        (vel.at[0, 0], v.at[0, X + 1, OWN, :]),
        (vel.at[1, :, pl.ds(127, 1), :], v.at[1, pl.ds(1, X), pl.ds(7, 1), :]),
        (vel.at[1, :, pl.ds(0, 1), :], v.at[1, pl.ds(1, X), pl.ds(136, 1), :]),
    ])
    three = pl.ds(0, 3)
    spin = Exchange(1, [
        (state.at[three, pl.ds(X - 2, 2)], q.at[three, pl.ds(0, 2), OWN, :]),
        (state.at[three, pl.ds(0, 2)], q.at[three, pl.ds(X + 2, 2), OWN, :]),
        (state.at[three, :, pl.ds(126, 2), :], q.at[three, all_x, pl.ds(6, 2), :]),
        (state.at[three, :, pl.ds(0, 2), :], q.at[three, all_x, pl.ds(136, 2), :]),
    ])
    dust = Exchange(2, [
        (q.at[3, pl.ds(X, 2), OWN, :], q.at[3, pl.ds(0, 2), OWN, :]),
        (q.at[3, pl.ds(2, 2), OWN, :], q.at[3, pl.ds(X + 2, 2), OWN, :]),
        (q.at[3, all_x, pl.ds(134, 2), :], q.at[3, all_x, pl.ds(6, 2), :]),
        (q.at[3, all_x, pl.ds(8, 2), :], q.at[3, all_x, pl.ds(136, 2), :]),
    ])

    def later(g, cs):
        return Exchange(g, [
            (q1v.at[cs, pl.ds(X - 2, 2), OWN, :], q1.at[cs, pl.ds(0, 2), OWN, :]),
            (q1v.at[cs, pl.ds(0, 2), OWN, :], q1.at[cs, pl.ds(X + 2, 2), OWN, :]),
            (q1v.at[cs, :, pl.ds(134, 2), :], q1.at[cs, all_x, pl.ds(6, 2), :]),
            (q1v.at[cs, :, pl.ds(8, 2), :], q1.at[cs, all_x, pl.ds(136, 2), :]),
        ])

    spin1 = later(3, three)
    dust1 = later(4, pl.ds(3, 1))

    barrier = pltpu.get_barrier_semaphore()

    def peer(j):
        return lax.rem(gx + j, GX)

    def greet(j, _):
        pl.semaphore_signal(barrier, inc=1, device_id={"gx": peer(j)}, device_id_type=MESH)
        return 0

    lax.fori_loop(1, GX, greet, 0)
    for n in (2, 3):
        @pl.when(target[n])
        def _(n=n):
            pl.semaphore_signal(barrier, inc=1, device_id=where[n], device_id_type=MESH)
    pl.semaphore_wait(
        barrier, GX - 1 + source[2].astype(jnp.int32) + source[3].astype(jnp.int32))

    wind.start()
    spin.start()

    clear_turned(qt)
    zero_plane = jnp.zeros((128, 128), f32)
    zeros[...] = jnp.zeros(zeros.shape, f32)
    zrows[...] = jnp.zeros(zrows.shape, f32)

    @pl.when(gx == 0)
    def _():
        v[0, 0, OWN, :] = zero_plane
        for c in range(4):
            for p in range(2):
                q[c, p, OWN, :] = zero_plane

    @pl.when(gx == GX - 1)
    def _():
        v[0, X + 1, OWN, :] = zero_plane
        for c in range(4):
            for p in range(2):
                q[c, X + 2 + p, OWN, :] = zero_plane

    def clear_rows(lo, vrow):
        def body(x, _):
            v[1, x + 1, pl.ds(vrow, 1), :] = jnp.zeros((1, 128), f32)
            for c in range(4):
                q[c, x + 2, pl.ds(lo, 2), :] = jnp.zeros((2, 128), f32)
            return 0
        lax.fori_loop(0, X, body, 0)

    @pl.when(gy == 0)
    def _():
        clear_rows(6, 7)

    @pl.when(gy == GY - 1)
    def _():
        clear_rows(136, 136)

    def edge(src, dst, n):
        return pltpu.make_async_copy(src, dst, out_sem.at[n])

    edges = [
        (gx == 0, edge(zeros, q1.at[:, pl.ds(0, 2), OWN, :], 0)),
        (gx == GX - 1, edge(zeros, q1.at[:, pl.ds(X + 2, 2), OWN, :], 1)),
        (gy == 0, edge(zrows, q1.at[:, all_x, pl.ds(6, 2), :], 2)),
        (gy == GY - 1, edge(zrows, q1.at[:, all_x, pl.ds(136, 2), :], 3)),
    ]
    for flag, copy in edges:
        pl.when(flag)(copy.start)

    loads[0].wait()
    loads[1].wait()

    def friction(g, _):
        for h in range(8):
            x = g * 8 + h
            east, north = v[0, x + 1, OWN, :], v[1, x + 1, OWN, :]
            levels = (east * east + north * north).T
            total = profile_weights[0] * levels[0:1]
            for level in range(1, 4):
                total = total + profile_weights[level] * levels[level:level + 1]
            stress[pl.ds(x, 1), :] = total
        return 0

    lax.fori_loop(0, X // 8, friction, 0)

    def column(row):
        spot = lax.broadcasted_iota(jnp.int32, (X, X), 0) == lax.broadcasted_iota(jnp.int32, (X, X), 1)
        return jnp.sum(jnp.where(spot, jnp.broadcast_to(row, (X, X)), 0.0), axis=1, keepdims=True)

    highest = lax.Precision.HIGHEST
    owner = tile[...].astype(f32)
    same = jnp.broadcast_to(owner, (X, X)) == column(owner)
    sooner = lax.broadcasted_iota(jnp.int32, (X, X), 0) < lax.broadcasted_iota(jnp.int32, (X, X), 1)
    rank = jnp.sum(jnp.where(same & sooner, 1.0, 0.0), axis=0, keepdims=True)
    slot = owner * 2.0 + rank
    placing = jnp.where(
        jnp.broadcast_to(slot, (2 * GX, X))
        == lax.broadcasted_iota(jnp.int32, (2 * GX, X), 0).astype(f32), 1.0, 0.0)
    packed[...] = jnp.dot(placing, stress[...], precision=highest, preferred_element_type=f32)

    def tiles_to(j):
        o = peer(j)
        return pltpu.make_async_remote_copy(
            src_ref=packed.at[pl.ds(2 * o, 2), :], dst_ref=got.at[pl.ds(2 * gx, 2), :],
            send_sem=a2a_sem.at[0], recv_sem=a2a_sem.at[1],
            device_id={"gx": o}, device_id_type=MESH)

    def rows_to(j):
        o = peer(j)
        return pltpu.make_async_remote_copy(
            src_ref=rows.at[pl.ds(o, 1), :], dst_ref=landed.at[pl.ds(gx, 1), :],
            send_sem=a2a_sem.at[2], recv_sem=a2a_sem.at[3],
            device_id={"gx": o}, device_id_type=MESH)

    def send_all(copy):
        def body(j, _):
            copy(j).start()
            return 0
        lax.fori_loop(1, GX, body, 0)

    def wait_all(ref, count, s):
        part = ref.at[pl.ds(0, count), :]
        pltpu.make_async_copy(part, part, a2a_sem.at[s]).wait()

    send_all(tiles_to)
    got[pl.ds(2 * gx, 2), :] = packed[pl.ds(2 * gx, 2), :]

    loads[2].wait()
    wind.wait_recv()

    def speeds(i, b):
        for k in range(N):
            wx[i, A(k), :] = SCALE * (v[0, i, S(k), :] + v[0, i + 1, S(k), :])
            wy[i, A(k), :] = SCALE * (v[1, i + 1, pl.ds(3 + k, 8, stride=N), :] + v[1, i + 1, S(k), :])
            wz[i, A(k), :] = SCALE * (qt[b, pl.ds(3 + k, 8, stride=N), :] + qt[b, S(k), :])

    def make_speeds(g, _):
        for b in range(8):
            qt[b, OWN, :] = v[2, g * 8 + b + 1, OWN, :].T
        for b in range(8):
            speeds(g * 8 + b, b)
        return 0

    lax.fori_loop(0, X // 8, make_speeds, 0)
    for k in range(N):
        wx[X, A(k), :] = SCALE * (v[0, X, S(k), :] + v[0, X + 1, S(k), :])
    winds_out = [pltpu.make_async_copy(a, b, out_sem.at[4 + n])
                 for n, (a, b) in enumerate(((wx, wxo), (wy, wyo), (wz, wzo)))]
    for copy in winds_out:
        copy.start()

    def parcels():
        wait_all(got, 2 * (GX - 1), 1)
        lifting = jnp.maximum(got[...] - thr[...], 0.0)
        flux = jnp.sum(lifting, axis=0, keepdims=True) / X
        flux_out[...] = flux
        reach = lax.broadcasted_iota(jnp.int32, (X, 128), 1).astype(f32) < column(count[...].astype(f32))
        masses = flux * share[...] * jnp.where(reach, 1.0, 0.0)
        going = jnp.where(
            jnp.broadcast_to(parcel[...], (GX, X)) == lax.broadcasted_iota(jnp.int32, (GX, X), 0), 1.0, 0.0)
        rows[...] = jnp.dot(going, masses, precision=highest, preferred_element_type=f32)
        send_all(rows_to)
        landed[pl.ds(gx, 1), :] = rows[pl.ds(gx, 1), :]

    def deposit():
        wait_all(landed, GX - 1, 3)
        loads[6].wait()
        top = lax.broadcasted_iota(jnp.int32, (128, 128), 0) == 0

        def body(g, _):
            for h in range(8):
                x = g * 8 + h
                drop = jnp.where(top, jnp.broadcast_to(landed[pl.ds(x, 1), :], (128, 128)), 0.0).T
                q[3, x + 2, OWN, :] = q[3, x + 2, OWN, :] + drop
            return 0

        lax.fori_loop(0, X // 8, body, 0)
        dust.start()

    def keep(c, x, u, value):
        q1v[c, x, S(u), :] = value

    def out_pair(comps, j):
        lo, hi = comps[0], comps[-1] + 1
        return pltpu.make_async_copy(
            q1v.at[pl.ds(lo, hi - lo), pl.ds(2 * j, 2), OWN, :],
            q1.at[pl.ds(lo, hi - lo), pl.ds(2 * j + 2, 2), OWN, :], out_sem.at[7 + lo])

    def sweep(groups, comps, extra):
        xstart(comps, q, wx, cx)
        zstart(groups, q, qt, zt, wz)

        def body(j, _):
            extra(j)
            sweep_step(j, groups, q, keep, wx, wy, wz, cx, qt, zt, az)
            out_pair(comps, j).start()
            return 0

        lax.fori_loop(0, PAIRS, body, 0)

    for c in range(3):
        loads[3 + c].wait()
    spin.wait_recv()

    def extra(j):
        pl.when(j == 4)(parcels)
        pl.when(j == 9)(deposit)

    clear_turned(qt)
    sweep(((0, 1, 2),), (0, 1, 2), extra)
    spin1.start()
    dust.wait_recv()
    sweep(((3,),), (3,), lambda j: None)
    dust1.start()

    for comps in ((0, 1, 2), (3,)):
        lo, hi = comps[0], comps[-1] + 1
        pltpu.make_async_copy(
            q1v.at[pl.ds(lo, hi - lo), :, OWN, :],
            q1.at[pl.ds(lo, hi - lo), all_x, OWN, :], out_sem.at[7 + lo]).wait()
    for copy in winds_out:
        copy.wait()
    for flag, copy in edges:
        pl.when(flag)(copy.wait)
    wait_all(packed, 2 * (GX - 1), 0)
    wait_all(rows, GX - 1, 2)
    wind.wait_send()
    spin.wait_send()
    dust.wait_send()
    spin1.wait_send()
    dust1.wait_send()
    spin1.wait_recv()
    dust1.wait_recv()


def second_kernel(q1, wxi, wyi, wzi, flux_in, out, flux_out, q, wx, wy, wz, ov, cx, qt, zt, az, sem, osem):
    def q_copy(j):
        return pltpu.make_async_copy(q1.at[:, pl.ds(2 * j, 2)], q.at[:, pl.ds(2 * j, 2)], sem.at[0, j])

    def w_copies(j):
        k = pl.ds(2 * j, 2)
        return [pltpu.make_async_copy(a.at[k], b.at[k], sem.at[1 + n, j])
                for n, (a, b) in enumerate(((wxi, wx), (wyi, wy), (wzi, wz)))]

    last = pltpu.make_async_copy(wxi.at[pl.ds(X, 1)], wx.at[pl.ds(X, 1)], sem.at[1, PAIRS])

    def begin(j, _):
        q_copy(j).start()
        for copy in w_copies(j):
            copy.start()
        return 0

    lax.fori_loop(0, PAIRS, begin, 0)
    q_copy(PAIRS).start()
    q_copy(PAIRS + 1).start()
    last.start()
    flux_out[...] = flux_in[...]
    clear_turned(qt)
    groups = ((0, 1), (2, 3))
    comps = (0, 1, 2, 3)
    for j in range(3):
        q_copy(j).wait()
    for copy in w_copies(0):
        copy.wait()

    def keep(c, x, u, value):
        ov[c, x, S(u), :] = value

    def out_pair(j):
        return pltpu.make_async_copy(
            ov.at[:, pl.ds(2 * j, 2), OWN, :], out.at[:, pl.ds(2 * j, 2)], osem.at[0])

    xstart(comps, q, wx, cx)
    zstart(groups, q, qt, zt, wz)

    def body(j, _):
        @pl.when(j < PAIRS - 1)
        def _():
            q_copy(j + 3).wait()
            for copy in w_copies(j + 1):
                copy.wait()

        @pl.when(j == PAIRS - 1)
        def _():
            last.wait()

        sweep_step(j, groups, q, keep, wx, wy, wz, cx, qt, zt, az)
        out_pair(j).start()
        return 0

    lax.fori_loop(0, PAIRS, body, 0)
    pltpu.make_async_copy(ov.at[:, :, OWN, :], out, osem.at[0]).wait()


def shards(state, velocity, threshold, tile_owner, parcel_owner, parcel_count, parcel_share):
    def vm(*shape):
        return pltpu.VMEM(shape, f32)

    def like(*shape):
        return jax.ShapeDtypeStruct(shape, f32)

    hbm = pl.BlockSpec(memory_space=pl.ANY)
    vmem = pl.BlockSpec(memory_space=pltpu.VMEM)
    work = [vm(4, 3, 8 * N, 128)] + [vm(8, ROWS, 128)] * 3
    speeds = [vm(X + 1, 8 * N, 128), vm(X, 8 * N, 128), vm(X, 8 * N, 128)]
    q1, wx, wy, wz, flux = pl.pallas_call(
        first_kernel,
        out_shape=(like(4, X + 4, ROWS, 128), like(X + 1, 8 * N, 128), like(X, 8 * N, 128),
                   like(X, 8 * N, 128), like(1, 128)),
        in_specs=[hbm, hbm] + [vmem] * 5,
        out_specs=(hbm, hbm, hbm, hbm, vmem),
        scratch_shapes=[vm(4, X + 4, ROWS, 128), vm(3, X + 2, ROWS, 128), vm(4, X, ROWS, 128)]
        + speeds + work
        + [vm(X, 128), vm(2 * GX, 128), vm(2 * GX, 128), vm(GX, 128), vm(GX, 128), vm(4, 2, 128, 128), vm(4, X, 2, 128),
           pltpu.SemaphoreType.DMA((7,)), pltpu.SemaphoreType.DMA((5, 4)), pltpu.SemaphoreType.DMA((5, 4)),
           pltpu.SemaphoreType.DMA((4,)), pltpu.SemaphoreType.DMA((11,))],
        compiler_params=pltpu.CompilerParams(
            collective_id=0, has_side_effects=True, vmem_limit_bytes=56 << 20),
    )(state, velocity, threshold, tile_owner.reshape(1, X), parcel_owner.reshape(1, X),
      parcel_count, parcel_share.reshape(X, 128))
    return pl.pallas_call(
        second_kernel,
        out_shape=(like(4, X, 128, 128), like(1, 128)),
        in_specs=[hbm] * 4 + [vmem],
        out_specs=(hbm, vmem),
        scratch_shapes=[vm(4, X + 4, ROWS, 128)] + speeds + [vm(4, X, ROWS, 128)] + work
        + [pltpu.SemaphoreType.DMA((4, PAIRS + 2)), pltpu.SemaphoreType.DMA((1,))],
        compiler_params=pltpu.CompilerParams(vmem_limit_bytes=56 << 20),
    )(q1, wx, wy, wz, flux)


def solution(mesh):
    return jax.shard_map(
        shards,
        mesh=mesh,
        in_specs=(
            P(None, "gx", "gy", None),
            P(None, "gx", "gy", None),
            P("gx", "gy"),
            P("gy", "gx", None),
            P("gy", "gx", None),
            P("gy", "gx"),
            P("gy", "gx", None),
        ),
        out_specs=(P(None, "gx", "gy", None), P("gx", "gy")),
        check_vma=False,
    )
```

```python
import jax
import jax.numpy as jnp
from jax import lax
from jax.experimental import pallas as pl
from jax.experimental.pallas import tpu as pltpu
from jax.sharding import PartitionSpec as P

MESH = pl.DeviceIdType.MESH
f32 = jnp.float32
profile_weights = (0.4, 0.3, 0.2, 0.1)
SCALE = 0.1 * 0.25
X = 32
PAIRS = X // 2
ROWS = 144
OWN = pl.ds(8, 128)
N = 17
GX, GY = 32, 4
PARCELS_AT, DEPOSIT_AT = 1, 6


def S(k):
    return pl.ds(4 + k, 8, stride=N)


def A(k):
    return pl.ds(8 * k, 8)


def minmod(a, b):
    return jnp.maximum(jnp.minimum(a, b), jnp.minimum(jnp.maximum(a, b), 0.0))


def rollup(v):
    return pltpu.roll(v, 7, 0)


def rolldn(v):
    return pltpu.roll(v, 1, 0)


class Line:
    def __init__(self, load):
        self.load = load
        v0, v15, v16 = load(0), load(15), load(16)
        wrap = rollup(v0) - v16
        before = v16 - v15
        twice = v16 + v16
        m = minmod(wrap, before)
        self.tail = (twice + m, twice - m, before)
        self.v = v0
        self.d = rolldn(wrap)
        self.l = rolldn(twice + m)
        self.f = None

    def step(self, k, w, mask):
        if k == 16:
            l, r, d = self.tail
        else:
            v = self.v
            ahead = self.load(k + 1)
            d = ahead - v if k < 15 else self.tail[2]
            if k % 2 == 0:
                self.clip = jnp.maximum(d, 0.0), jnp.minimum(d, 0.0)
                m = jnp.maximum(jnp.minimum(self.d, self.clip[0]), self.clip[1])
            else:
                m = jnp.maximum(jnp.minimum(d, self.clip[0]), self.clip[1])
            twice = v + v
            l, r = twice + m, twice - m
            self.v = ahead
        f = w * jnp.where(mask, self.l, r)
        out = None if self.f is None else f - self.f
        if k == 0:
            self.first = rollup(f)
        self.f, self.l, self.d = f, l, d
        return out

    def end(self):
        return self.first - self.f


def turn_in(i, c, b, q, qt):
    qt[2 * c + b, OWN, :] = q[c, i + 2 + b, OWN, :].T


def turn_out(c, b, zt, az):
    az[2 * c + b, OWN, :] = zt[2 * c + b, OWN, :].T


def zplane(i, b, comps, qt, zt, wz):
    lines = {c: Line(lambda k, c=c: qt[2 * c + b, S(k), :]) for c in comps}
    for k in range(N):
        w = wz[i + b, A(k), :]
        mask = w > 0
        for c in comps:
            out = lines[c].step(k, w, mask)
            if k:
                zt[2 * c + b, S(k - 1), :] = out
    for c in comps:
        zt[2 * c + b, S(16), :] = lines[c].end()


def xypair(i, comps, q, write, wx, wy, az, cx):
    lines = {
        (c, b): Line(lambda k, c=c, b=b: q[c, i + 2 + b, S(k), :]) for c in comps for b in range(2)
    }
    for k in range(N + 1):
        acc = {}
        if k < N:
            for b in range(2):
                w = wy[i + b, A(k), :]
                mask = w > 0
                for c in comps:
                    acc[c, b] = lines[c, b].step(k, w, mask)
        else:
            for key, line in lines.items():
                acc[key] = line.end()
        if k == 0:
            continue
        u = k - 1
        w0 = wx[i + 1, A(u), :]
        w1 = wx[i + 2, A(u), :]
        m0, m1 = w0 > 0, w1 > 0
        for c in comps:
            q1 = q[c, i + 3, S(u), :]
            q2 = q[c, i + 4, S(u), :]
            db = q2 - q1
            dc = q[c, i + 5, S(u), :] - q2
            high, low = jnp.maximum(db, 0.0), jnp.minimum(db, 0.0)
            s1 = jnp.maximum(jnp.minimum(cx[c, 0, A(u), :], high), low)
            s2 = jnp.maximum(jnp.minimum(dc, high), low)
            t1 = q1 + q1
            t2 = q2 + q2
            f0 = w0 * jnp.where(m0, cx[c, 1, A(u), :], t1 - s1)
            f1 = w1 * jnp.where(m1, t1 + s1, t2 - s2)
            fm = cx[c, 2, A(u), :]
            cx[c, 0, A(u), :] = dc
            cx[c, 1, A(u), :] = t2 + s2
            cx[c, 2, A(u), :] = f1
            write(c, i, u, q[c, i + 2, S(u), :] - ((f0 - fm) + (acc[c, 0] + az[2 * c, S(u), :])))
            write(c, i + 1, u, q1 - ((f1 - f0) + (acc[c, 1] + az[2 * c + 1, S(u), :])))


def xstart(i, comps, q, wx, cx):
    for u in range(N):
        w = wx[i, A(u), :]
        mask = w > 0
        for c in comps:
            qa, qb, qc, qd = (q[c, i + p, S(u), :] for p in range(4))
            db, dc = qc - qb, qd - qc
            left = (qb + qb) + minmod(qb - qa, db)
            m = minmod(db, dc)
            twice = qc + qc
            cx[c, 0, A(u), :] = dc
            cx[c, 1, A(u), :] = twice + m
            cx[c, 2, A(u), :] = w * jnp.where(mask, left, twice - m)


def sweep(groups, q, write, wx, wy, wz, cx, qt, zt, az, first, before, after):
    comps = [c for group in groups for c in group]

    def pair(j):
        return lax.rem(j + first, PAIRS)

    for group in groups:
        for b in range(2):
            for c in group:
                turn_in(2 * first, c, b, q, qt)
    for group in groups:
        for b in range(2):
            zplane(2 * first, b, group, qt, zt, wz)
            for c in group:
                turn_in(2 * first + 2, c, b, q, qt)
    xstart(2 * first, comps, q, wx, cx)

    def body(j, _):
        before(j)
        if first:
            pl.when(j == PAIRS - first)(lambda: xstart(0, comps, q, wx, cx))
        for group in groups:
            for b in range(2):
                for c in group:
                    turn_out(c, b, zt, az)
        for group in groups:
            for b in range(2):
                zplane(2 * pair(j + 1), b, group, qt, zt, wz)
                for c in group:
                    turn_in(2 * pair(j + 2), c, b, q, qt)
        for group in groups:
            xypair(2 * pair(j), group, q, write, wx, wy, az, cx)
        after(pair(j))
        return 0

    lax.fori_loop(0, PAIRS, body, 0)


def clear_turned(qt):
    zero = jnp.zeros((8, 128), f32)
    for s in range(8):
        qt[s, 0:8, :] = zero
        qt[s, 136:144, :] = zero


def first_kernel(
    state, vel, thr_in, tile_in, parcel_in, count_in, share_in,
    q1, wx, wy, wz, ov, flux_out,
    q, v, yh, cx, qt, zt, az, stress, packed, got, rows, landed, thr, tile, parcel, count, share,
    load_sem, lsend, lrecv, a2a_sem,
):
    gx, gy = lax.axis_index("gx"), lax.axis_index("gy")

    def local(src, dst, s):
        return pltpu.make_async_copy(src, dst, load_sem.at[s])

    loads = [
        local(vel.at[a], v.at[a, pl.ds(1, X), OWN, :], a) for a in range(3)
    ] + [local(state.at[c], q.at[c, pl.ds(2, X), OWN, :], 3 + c) for c in range(4)]
    loads[0].start()
    loads[1].start()
    small = [local(src, dst, 7 + n) for n, (src, dst) in enumerate(
        ((tile_in, tile), (thr_in, thr), (parcel_in, parcel), (count_in, count), (share_in, share)))]
    for copy in small:
        copy.start()

    target = (gx < GX - 1, gx > 0, gy < GY - 1, gy > 0)
    source = (gx > 0, gx < GX - 1, gy > 0, gy < GY - 1)
    where = (
        {"gx": lax.rem(gx + 1, GX)},
        {"gx": lax.rem(gx + GX - 1, GX)},
        {"gy": lax.rem(gy + 1, GY)},
        {"gy": lax.rem(gy + GY - 1, GY)},
    )
    along_x, along_y, both = (0, 1), (2, 3), (0, 1, 2, 3)

    class Exchange:
        def __init__(self, g, pieces):
            self.copies = [
                pltpu.make_async_remote_copy(
                    src_ref=src, dst_ref=dst, send_sem=lsend.at[g, n], recv_sem=lrecv.at[g, n],
                    device_id=where[n], device_id_type=MESH,
                )
                for n, (src, dst) in enumerate(pieces)
            ]

        def start(self, ways):
            for n in ways:
                pl.when(target[n])(self.copies[n].start)

        def wait_recv(self, ways):
            for n in ways:
                pl.when(source[n])(self.copies[n].wait_recv)

        def wait_send(self):
            for n in both:
                pl.when(target[n])(self.copies[n].wait_send)

    all_x = pl.ds(2, X)
    wind = Exchange(0, [
        (vel.at[0, X - 1], v.at[0, 0, OWN, :]),
        (vel.at[0, 0], v.at[0, X + 1, OWN, :]),
        (vel.at[1, :, pl.ds(127, 1), :], v.at[1, pl.ds(1, X), pl.ds(7, 1), :]),
        (vel.at[1, :, pl.ds(0, 1), :], v.at[1, pl.ds(1, X), pl.ds(136, 1), :]),
    ])
    three = pl.ds(0, 3)
    spin = Exchange(1, [
        (state.at[three, pl.ds(X - 2, 2)], q.at[three, pl.ds(0, 2), OWN, :]),
        (state.at[three, pl.ds(0, 2)], q.at[three, pl.ds(X + 2, 2), OWN, :]),
        (state.at[three, :, pl.ds(126, 2), :], q.at[three, all_x, pl.ds(6, 2), :]),
        (state.at[three, :, pl.ds(0, 2), :], q.at[three, all_x, pl.ds(136, 2), :]),
    ])
    dust = Exchange(2, [
        (q.at[3, pl.ds(X, 2), OWN, :], q.at[3, pl.ds(0, 2), OWN, :]),
        (q.at[3, pl.ds(2, 2), OWN, :], q.at[3, pl.ds(X + 2, 2), OWN, :]),
        (q.at[3, all_x, pl.ds(134, 2), :], q.at[3, all_x, pl.ds(6, 2), :]),
        (q.at[3, all_x, pl.ds(8, 2), :], q.at[3, all_x, pl.ds(136, 2), :]),
    ])
    second = [
        Exchange(3 + c, [
            (q1.at[c, pl.ds(X, 2), OWN, :], q1.at[c, pl.ds(0, 2), OWN, :]),
            (q1.at[c, pl.ds(2, 2), OWN, :], q1.at[c, pl.ds(X + 2, 2), OWN, :]),
            (q1.at[c, all_x, pl.ds(134, 2), :], yh.at[0, c]),
            (q1.at[c, all_x, pl.ds(8, 2), :], yh.at[1, c]),
        ])
        for c in range(4)
    ]

    barrier = pltpu.get_barrier_semaphore()

    def peer(j):
        return lax.rem(gx + j, GX)

    def greet(j, _):
        pl.semaphore_signal(barrier, inc=1, device_id={"gx": peer(j)}, device_id_type=MESH)
        return 0

    lax.fori_loop(1, GX, greet, 0)
    for n in along_y:
        @pl.when(target[n])
        def _(n=n):
            pl.semaphore_signal(barrier, inc=1, device_id=where[n], device_id_type=MESH)

    clear_turned(qt)
    zero_plane = jnp.zeros((128, 128), f32)

    def clear_planes(vp, p0):
        v[0, vp, OWN, :] = zero_plane
        for c in range(4):
            for p in range(2):
                q[c, p0 + p, OWN, :] = zero_plane
                q1[c, p0 + p, OWN, :] = zero_plane

    pl.when(gx == 0)(lambda: clear_planes(0, 0))
    pl.when(gx == GX - 1)(lambda: clear_planes(X + 1, X + 2))

    def clear_rows(side, lo, vrow):
        def body(x, _):
            v[1, x + 1, pl.ds(vrow, 1), :] = jnp.zeros((1, 128), f32)
            for c in range(4):
                q[c, x + 2, pl.ds(lo, 2), :] = jnp.zeros((2, 128), f32)
                yh[side, c, x] = jnp.zeros((2, 128), f32)
            return 0
        lax.fori_loop(0, X, body, 0)

    pl.when(gy == 0)(lambda: clear_rows(0, 6, 7))
    pl.when(gy == GY - 1)(lambda: clear_rows(1, 136, 136))

    loads[0].wait()
    loads[1].wait()
    for copy in loads[2:]:
        copy.start()

    def friction(g, _):
        for h in range(8):
            x = g * 8 + h
            east, north = v[0, x + 1, OWN, :], v[1, x + 1, OWN, :]
            levels = (east * east + north * north).T
            total = profile_weights[0] * levels[0:1]
            for level in range(1, 4):
                total = total + profile_weights[level] * levels[level:level + 1]
            stress[pl.ds(x, 1), :] = total
        return 0

    lax.fori_loop(0, X // 8, friction, 0)

    def column(row):
        spot = lax.broadcasted_iota(jnp.int32, (X, X), 0) == lax.broadcasted_iota(jnp.int32, (X, X), 1)
        return jnp.sum(jnp.where(spot, jnp.broadcast_to(row, (X, X)), 0.0), axis=1, keepdims=True)

    highest = lax.Precision.HIGHEST
    for copy in small:
        copy.wait()
    owner = tile[...].astype(f32)
    same = jnp.broadcast_to(owner, (X, X)) == column(owner)
    sooner = lax.broadcasted_iota(jnp.int32, (X, X), 0) < lax.broadcasted_iota(jnp.int32, (X, X), 1)
    rank = jnp.sum(jnp.where(same & sooner, 1.0, 0.0), axis=0, keepdims=True)
    slot = owner * 2.0 + rank
    placing = jnp.where(
        jnp.broadcast_to(slot, (2 * GX, X))
        == lax.broadcasted_iota(jnp.int32, (2 * GX, X), 0).astype(f32), 1.0, 0.0)
    packed[...] = jnp.dot(placing, stress[...], precision=highest, preferred_element_type=f32)

    def tiles_to(j):
        o = peer(j)
        return pltpu.make_async_remote_copy(
            src_ref=packed.at[pl.ds(2 * o, 2), :], dst_ref=got.at[pl.ds(2 * gx, 2), :],
            send_sem=a2a_sem.at[0], recv_sem=a2a_sem.at[1],
            device_id={"gx": o}, device_id_type=MESH)

    def rows_to(j):
        o = peer(j)
        return pltpu.make_async_remote_copy(
            src_ref=rows.at[pl.ds(o, 1), :], dst_ref=landed.at[pl.ds(gx, 1), :],
            send_sem=a2a_sem.at[2], recv_sem=a2a_sem.at[3],
            device_id={"gx": o}, device_id_type=MESH)

    def send_all(copy):
        def body(j, _):
            copy(j).start()
            return 0
        lax.fori_loop(1, GX, body, 0)

    def wait_all(ref, count, s):
        part = ref.at[pl.ds(0, count), :]
        pltpu.make_async_copy(part, part, a2a_sem.at[s]).wait()

    pl.semaphore_wait(
        barrier, GX - 1 + source[2].astype(jnp.int32) + source[3].astype(jnp.int32))
    send_all(tiles_to)
    wind.start(along_y)
    spin.start(along_y)
    spin.start(along_x)
    wind.start(along_x)
    got[pl.ds(2 * gx, 2), :] = packed[pl.ds(2 * gx, 2), :]

    def speed_x(i):
        for k in range(N):
            wx[i, A(k), :] = SCALE * (v[0, i, S(k), :] + v[0, i + 1, S(k), :])

    def speeds_x(i, _):
        speed_x(i)
        return 0

    lax.fori_loop(1, X, speeds_x, 0)
    loads[2].wait()

    def below(k):
        return pl.ds(3 + k, 8, stride=N)

    def speeds_z(g, _):
        for b in range(8):
            qt[b, OWN, :] = v[2, g * 8 + b + 1, OWN, :].T
        for b in range(8):
            for k in range(N):
                wz[g * 8 + b, A(k), :] = SCALE * (qt[b, below(k), :] + qt[b, S(k), :])
        return 0

    lax.fori_loop(0, X // 8, speeds_z, 0)
    wind.wait_recv(along_y)

    def speeds_y(i, _):
        for k in range(N):
            wy[i, A(k), :] = SCALE * (v[1, i + 1, below(k), :] + v[1, i + 1, S(k), :])
        return 0

    lax.fori_loop(0, X, speeds_y, 0)

    def parcels():
        wait_all(got, 2 * (GX - 1), 1)
        lifting = jnp.maximum(got[...] - thr[...], 0.0)
        flux = jnp.sum(lifting, axis=0, keepdims=True) / X
        flux_out[...] = flux
        reach = lax.broadcasted_iota(jnp.int32, (X, 128), 1).astype(f32) < column(count[...].astype(f32))
        masses = flux * share[...] * jnp.where(reach, 1.0, 0.0)
        going = jnp.where(
            jnp.broadcast_to(parcel[...], (GX, X)) == lax.broadcasted_iota(jnp.int32, (GX, X), 0), 1.0, 0.0)
        rows[...] = jnp.dot(going, masses, precision=highest, preferred_element_type=f32)
        send_all(rows_to)
        landed[pl.ds(gx, 1), :] = rows[pl.ds(gx, 1), :]

    def deposit():
        wait_all(landed, GX - 1, 3)
        loads[6].wait()
        top = lax.broadcasted_iota(jnp.int32, (128, 128), 0) == 0

        def body(g, _):
            for h in range(8):
                x = g * 8 + h
                drop = jnp.where(top, jnp.broadcast_to(landed[pl.ds(x, 1), :], (128, 128)), 0.0).T
                q[3, x + 2, OWN, :] = q[3, x + 2, OWN, :] + drop
            return 0

        lax.fori_loop(0, X // 8, body, 0)
        dust.start(along_y)
        dust.start(along_x)

    def patch(c):
        def body(x, _):
            q1[c, x + 2, pl.ds(6, 2), :] = yh[0, c, x]
            q1[c, x + 2, pl.ds(136, 2), :] = yh[1, c, x]
            return 0
        lax.fori_loop(0, X, body, 0)

    def keep(c, x, u, value):
        q1[c, x + 2, S(u), :] = value

    def keep_last(c, x, u, value):
        ov[x, S(u), :] = value

    work = (wx, wy, wz, cx, qt, zt, az)
    nothing = lambda j: None

    def edges_come():
        spin.wait_recv(along_x)
        wind.wait_recv(along_x)
        speed_x(0)
        speed_x(X)

    def spin_before(j):
        pl.when(j == PARCELS_AT)(parcels)
        pl.when(j == DEPOSIT_AT)(deposit)
        pl.when(j == PAIRS - 2)(edges_come)

    for c in range(3):
        loads[3 + c].wait()
    spin.wait_recv(along_y)
    sweep(((0, 1, 2),), q, keep, *work, 1, spin_before, nothing)
    for c in range(3):
        second[c].start(along_y)
        second[c].start(along_x)
    dust.wait_recv(along_y)
    sweep(((3,),), q, keep, *work, 1,
          lambda j: pl.when(j == PAIRS - 2)(lambda: dust.wait_recv(along_x)), nothing)
    second[3].start(along_y)
    second[3].start(along_x)
    second[0].wait_recv(along_y)
    patch(0)
    sweep(((0,),), q1, keep_last, *work, 1,
          lambda j: pl.when(j == PAIRS - 2)(lambda: second[0].wait_recv(along_x)), nothing)
    for c in range(1, 4):
        second[c].wait_recv(along_y)
        patch(c)
        second[c].wait_recv(along_x)

    wait_all(packed, 2 * (GX - 1), 0)
    wait_all(rows, GX - 1, 2)
    for exchange in [wind, spin, dust] + second:
        exchange.wait_send()


def second_kernel(q1, wx, wy, wz, ov0, flux_in, out, flux_out, ov, cx, qt, zt, az, osem):
    ready = pltpu.make_async_copy(ov0.at[:, OWN, :], out.at[0], osem.at[1])
    ready.start()
    flux_out[...] = flux_in[...]
    clear_turned(qt)

    def keep(c, x, u, value):
        ov[c - 1, x, S(u), :] = value

    def out_pair(j):
        pltpu.make_async_copy(
            ov.at[:, pl.ds(2 * j, 2), OWN, :], out.at[pl.ds(1, 3), pl.ds(2 * j, 2)], osem.at[0]).start()

    sweep(((1, 2, 3),), q1, keep, wx, wy, wz, cx, qt, zt, az, 0, lambda j: None, out_pair)
    pltpu.make_async_copy(ov.at[:, :, OWN, :], out.at[pl.ds(1, 3)], osem.at[0]).wait()
    ready.wait()


def shards(state, velocity, threshold, tile_owner, parcel_owner, parcel_count, parcel_share):
    def vm(*shape):
        return pltpu.VMEM(shape, f32)

    def like(*shape):
        return jax.ShapeDtypeStruct(shape, f32)

    hbm = pl.BlockSpec(memory_space=pltpu.HBM)

    def far(x):
        return pltpu.with_memory_space_constraint(x, pltpu.HBM)

    vmem = pl.BlockSpec(memory_space=pltpu.VMEM)
    work = [vm(4, 3, 8 * N, 128)] + [vm(8, ROWS, 128)] * 3
    *between, flux = pl.pallas_call(
        first_kernel,
        out_shape=(vm(4, X + 4, ROWS, 128), vm(X + 1, 8 * N, 128), vm(X, 8 * N, 128),
                   vm(X, 8 * N, 128), vm(X, ROWS, 128), like(1, 128)),
        in_specs=[hbm] * 7,
        out_specs=(vmem,) * 6,
        scratch_shapes=[vm(4, X + 4, ROWS, 128), vm(3, X + 2, ROWS, 128), vm(2, 4, X, 2, 128)]
        + work
        + [vm(X, 128), vm(2 * GX, 128), vm(2 * GX, 128), vm(GX, 128), vm(GX, 128),
           vm(1, 128)] + [pltpu.VMEM((1, X), jnp.int32)] * 3 + [vm(X, 128),
           pltpu.SemaphoreType.DMA((12,)), pltpu.SemaphoreType.DMA((7, 4)), pltpu.SemaphoreType.DMA((7, 4)),
           pltpu.SemaphoreType.DMA((4,))],
        compiler_params=pltpu.CompilerParams(
            collective_id=0, has_side_effects=True, vmem_limit_bytes=24 << 20),
    )(*map(far, (state, velocity, threshold, tile_owner.reshape(1, X), parcel_owner.reshape(1, X),
                 parcel_count, parcel_share.reshape(X, 128))))
    return pl.pallas_call(
        second_kernel,
        out_shape=(like(4, X, 128, 128), like(1, 128)),
        in_specs=[vmem] * 6,
        out_specs=(hbm, vmem),
        scratch_shapes=[vm(3, X, ROWS, 128)] + work + [pltpu.SemaphoreType.DMA((2,))],
        compiler_params=pltpu.CompilerParams(vmem_limit_bytes=16 << 20),
    )(*between, flux)


def solution(mesh):
    return jax.shard_map(
        shards,
        mesh=mesh,
        in_specs=(
            P(None, "gx", "gy", None),
            P(None, "gx", "gy", None),
            P("gx", "gy"),
            P("gy", "gx", None),
            P("gy", "gx", None),
            P("gy", "gx"),
            P("gy", "gx", None),
        ),
        out_specs=(P(None, "gx", "gy", None), P("gx", "gy")),
        check_vma=False,
    )
```

```python
import jax
import jax.numpy as jnp
from jax import lax
from jax.experimental import pallas as pl
from jax.experimental.pallas import tpu as pltpu
from jax.sharding import PartitionSpec as P

MESH = pl.DeviceIdType.MESH
f32 = jnp.float32
profile_weights = (0.4, 0.3, 0.2, 0.1)
SCALE = 0.1 * 0.25
X = 32
PAIRS = X // 2
ROWS = 144
OWN = pl.ds(8, 128)
N = 17
GX, GY = 32, 4
PARCELS_AT, DEPOSIT_AT = 4, 11


def S(k):
    return pl.ds(4 + k, 8, stride=N)


def A(k):
    return pl.ds(8 * k, 8)


def minmod(a, b):
    return jnp.maximum(jnp.minimum(a, b), jnp.minimum(jnp.maximum(a, b), 0.0))


def rollup(v):
    return pltpu.roll(v, 7, 0)


def rolldn(v):
    return pltpu.roll(v, 1, 0)


class Line:
    def __init__(self, load):
        self.load = load
        v0, v15, v16 = load(0), load(15), load(16)
        wrap = rollup(v0) - v16
        before = v16 - v15
        twice = v16 + v16
        m = minmod(wrap, before)
        self.tail = (twice + m, twice - m, before)
        self.v = v0
        self.d = rolldn(wrap)
        self.l = rolldn(twice + m)
        self.f = None

    def step(self, k, w, mask):
        if k == 16:
            l, r, d = self.tail
        else:
            v = self.v
            ahead = self.load(k + 1)
            d = ahead - v if k < 15 else self.tail[2]
            if k % 2 == 0:
                self.clip = jnp.maximum(d, 0.0), jnp.minimum(d, 0.0)
                m = jnp.maximum(jnp.minimum(self.d, self.clip[0]), self.clip[1])
            else:
                m = jnp.maximum(jnp.minimum(d, self.clip[0]), self.clip[1])
            twice = v + v
            l, r = twice + m, twice - m
            self.v = ahead
        f = w * jnp.where(mask, self.l, r)
        out = None if self.f is None else f - self.f
        if k == 0:
            self.first = rollup(f)
        self.f, self.l, self.d = f, l, d
        return out

    def end(self):
        return self.first - self.f


def turn_in(i, c, b, q, qt):
    qt[2 * c + b, OWN, :] = q[c, i + 2 + b, OWN, :].T


def turn_out(c, b, zt, az):
    az[2 * c + b, OWN, :] = zt[2 * c + b, OWN, :].T


def zplane(i, b, comps, qt, zt, wz):
    lines = {c: Line(lambda k, c=c: qt[2 * c + b, S(k), :]) for c in comps}
    for k in range(N):
        w = wz[i + b, A(k), :]
        mask = w > 0
        for c in comps:
            out = lines[c].step(k, w, mask)
            if k:
                zt[2 * c + b, S(k - 1), :] = out
    for c in comps:
        zt[2 * c + b, S(16), :] = lines[c].end()


def xypair(i, comps, q, write, wx, wy, az, cx):
    lines = {
        (c, b): Line(lambda k, c=c, b=b: q[c, i + 2 + b, S(k), :]) for c in comps for b in range(2)
    }
    for k in range(N + 1):
        acc = {}
        if k < N:
            for b in range(2):
                w = wy[i + b, A(k), :]
                mask = w > 0
                for c in comps:
                    acc[c, b] = lines[c, b].step(k, w, mask)
        else:
            for key, line in lines.items():
                acc[key] = line.end()
        if k == 0:
            continue
        u = k - 1
        w0 = wx[i + 1, A(u), :]
        w1 = wx[i + 2, A(u), :]
        m0, m1 = w0 > 0, w1 > 0
        for c in comps:
            q1 = q[c, i + 3, S(u), :]
            q2 = q[c, i + 4, S(u), :]
            db = q2 - q1
            dc = q[c, i + 5, S(u), :] - q2
            high, low = jnp.maximum(db, 0.0), jnp.minimum(db, 0.0)
            s1 = jnp.maximum(jnp.minimum(cx[c, 0, A(u), :], high), low)
            s2 = jnp.maximum(jnp.minimum(dc, high), low)
            t1 = q1 + q1
            t2 = q2 + q2
            f0 = w0 * jnp.where(m0, cx[c, 1, A(u), :], t1 - s1)
            f1 = w1 * jnp.where(m1, t1 + s1, t2 - s2)
            fm = cx[c, 2, A(u), :]
            cx[c, 0, A(u), :] = dc
            cx[c, 1, A(u), :] = t2 + s2
            cx[c, 2, A(u), :] = f1
            write(c, i, u, q[c, i + 2, S(u), :] - ((f0 - fm) + (acc[c, 0] + az[2 * c, S(u), :])))
            write(c, i + 1, u, q1 - ((f1 - f0) + (acc[c, 1] + az[2 * c + 1, S(u), :])))


def xstart(i, comps, q, wx, cx):
    for u in range(N):
        w = wx[i, A(u), :]
        mask = w > 0
        for c in comps:
            qa, qb, qc, qd = (q[c, i + p, S(u), :] for p in range(4))
            db, dc = qc - qb, qd - qc
            left = (qb + qb) + minmod(qb - qa, db)
            m = minmod(db, dc)
            twice = qc + qc
            cx[c, 0, A(u), :] = dc
            cx[c, 1, A(u), :] = twice + m
            cx[c, 2, A(u), :] = w * jnp.where(mask, left, twice - m)


def sweep(groups, q, write, wx, wy, wz, cx, qt, zt, az, first, before, after):
    comps = [c for group in groups for c in group]

    def pair(j):
        return lax.rem(j + first, PAIRS)

    for group in groups:
        for b in range(2):
            for c in group:
                turn_in(2 * first, c, b, q, qt)
    for group in groups:
        for b in range(2):
            zplane(2 * first, b, group, qt, zt, wz)
            for c in group:
                turn_in(2 * first + 2, c, b, q, qt)
    xstart(2 * first, comps, q, wx, cx)

    def body(j, _):
        before(j)
        if first:
            pl.when(j == PAIRS - first)(lambda: xstart(0, comps, q, wx, cx))
        for group in groups:
            for b in range(2):
                for c in group:
                    turn_out(c, b, zt, az)
        for group in groups:
            for b in range(2):
                zplane(2 * pair(j + 1), b, group, qt, zt, wz)
                for c in group:
                    turn_in(2 * pair(j + 2), c, b, q, qt)
        for group in groups:
            xypair(2 * pair(j), group, q, write, wx, wy, az, cx)
        after(pair(j))
        return 0

    lax.fori_loop(0, PAIRS, body, 0)


def clear_turned(qt):
    zero = jnp.zeros((8, 128), f32)
    for s in range(8):
        qt[s, 0:8, :] = zero
        qt[s, 136:144, :] = zero


def first_kernel(
    state, vel, thr_in, tile_in, parcel_in, count_in, share_in,
    q1, wx, wy, wz, ov, flux_out,
    q, v, yh, cx, qt, zt, az, stress, packed, got, rows, landed, thr, tile, parcel, count, share,
    load_sem, lsend, lrecv, a2a_sem,
):
    gx, gy = lax.axis_index("gx"), lax.axis_index("gy")

    def local(src, dst, s):
        return pltpu.make_async_copy(src, dst, load_sem.at[s])

    def winds(g):
        return local(vel.at[:, pl.ds(8 * g, 8)], v.at[:, pl.ds(8 * g + 1, 8), OWN, :], g)

    loads = [local(state.at[c], q.at[c, pl.ds(2, X), OWN, :], 4 + c) for c in range(4)]
    for g in range(X // 8):
        winds(g).start()
    small = [local(src, dst, 8 + n) for n, (src, dst) in enumerate(
        ((tile_in, tile), (thr_in, thr), (parcel_in, parcel), (count_in, count), (share_in, share)))]
    for copy in small:
        copy.start()

    target = (gx < GX - 1, gx > 0, gy < GY - 1, gy > 0)
    source = (gx > 0, gx < GX - 1, gy > 0, gy < GY - 1)
    where = (
        {"gx": lax.rem(gx + 1, GX)},
        {"gx": lax.rem(gx + GX - 1, GX)},
        {"gy": lax.rem(gy + 1, GY)},
        {"gy": lax.rem(gy + GY - 1, GY)},
    )
    along_x, along_y, both = (0, 1), (2, 3), (0, 1, 2, 3)

    class Exchange:
        def __init__(self, g, pieces):
            self.copies = [
                pltpu.make_async_remote_copy(
                    src_ref=src, dst_ref=dst, send_sem=lsend.at[g, n], recv_sem=lrecv.at[g, n],
                    device_id=where[n], device_id_type=MESH,
                )
                for n, (src, dst) in enumerate(pieces)
            ]

        def start(self, ways):
            for n in ways:
                pl.when(target[n])(self.copies[n].start)

        def wait_recv(self, ways):
            for n in ways:
                pl.when(source[n])(self.copies[n].wait_recv)

        def wait_send(self):
            for n in both:
                pl.when(target[n])(self.copies[n].wait_send)

    all_x = pl.ds(2, X)
    wind = Exchange(0, [
        (vel.at[0, X - 1], v.at[0, 0, OWN, :]),
        (vel.at[0, 0], v.at[0, X + 1, OWN, :]),
        (vel.at[1, :, pl.ds(127, 1), :], v.at[1, pl.ds(1, X), pl.ds(7, 1), :]),
        (vel.at[1, :, pl.ds(0, 1), :], v.at[1, pl.ds(1, X), pl.ds(136, 1), :]),
    ])
    spin = [
        Exchange(7 + c, [
            (state.at[c, pl.ds(X - 2, 2)], q.at[c, pl.ds(0, 2), OWN, :]),
            (state.at[c, pl.ds(0, 2)], q.at[c, pl.ds(X + 2, 2), OWN, :]),
            (state.at[c, :, pl.ds(126, 2), :], q.at[c, all_x, pl.ds(6, 2), :]),
            (state.at[c, :, pl.ds(0, 2), :], q.at[c, all_x, pl.ds(136, 2), :]),
        ])
        for c in range(3)
    ]
    dust = Exchange(2, [
        (q.at[3, pl.ds(X, 2), OWN, :], q.at[3, pl.ds(0, 2), OWN, :]),
        (q.at[3, pl.ds(2, 2), OWN, :], q.at[3, pl.ds(X + 2, 2), OWN, :]),
        (q.at[3, all_x, pl.ds(134, 2), :], q.at[3, all_x, pl.ds(6, 2), :]),
        (q.at[3, all_x, pl.ds(8, 2), :], q.at[3, all_x, pl.ds(136, 2), :]),
    ])
    second = [
        Exchange(3 + c, [
            (q1.at[c, pl.ds(X, 2), OWN, :], q1.at[c, pl.ds(0, 2), OWN, :]),
            (q1.at[c, pl.ds(2, 2), OWN, :], q1.at[c, pl.ds(X + 2, 2), OWN, :]),
            (q1.at[c, all_x, pl.ds(134, 2), :], yh.at[0, c]),
            (q1.at[c, all_x, pl.ds(8, 2), :], yh.at[1, c]),
        ])
        for c in range(4)
    ]

    barrier = pltpu.get_barrier_semaphore()

    def peer(j):
        return lax.rem(gx + j, GX)

    def greet(j, _):
        pl.semaphore_signal(barrier, inc=1, device_id={"gx": peer(j)}, device_id_type=MESH)
        return 0

    lax.fori_loop(1, GX, greet, 0)
    for n in along_y:
        @pl.when(target[n])
        def _(n=n):
            pl.semaphore_signal(barrier, inc=1, device_id=where[n], device_id_type=MESH)

    clear_turned(qt)
    zero_plane = jnp.zeros((128, 128), f32)

    def clear_planes(vp, p0):
        v[0, vp, OWN, :] = zero_plane
        for c in range(4):
            for p in range(2):
                q[c, p0 + p, OWN, :] = zero_plane
                q1[c, p0 + p, OWN, :] = zero_plane

    pl.when(gx == 0)(lambda: clear_planes(0, 0))
    pl.when(gx == GX - 1)(lambda: clear_planes(X + 1, X + 2))

    def clear_rows(side, lo, vrow):
        def body(x, _):
            v[1, x + 1, pl.ds(vrow, 1), :] = jnp.zeros((1, 128), f32)
            for c in range(4):
                q[c, x + 2, pl.ds(lo, 2), :] = jnp.zeros((2, 128), f32)
                yh[side, c, x] = jnp.zeros((2, 128), f32)
            return 0
        lax.fori_loop(0, X, body, 0)

    pl.when(gy == 0)(lambda: clear_rows(0, 6, 7))
    pl.when(gy == GY - 1)(lambda: clear_rows(1, 136, 136))

    pl.semaphore_wait(
        barrier, GX - 1 + source[2].astype(jnp.int32) + source[3].astype(jnp.int32))
    wind.start(along_y)
    for c in range(3):
        spin[c].start(along_y)


    def below(k):
        return pl.ds(3 + k, 8, stride=N)

    def speed_x(i):
        for k in range(N):
            wx[i, A(k), :] = SCALE * (v[0, i, S(k), :] + v[0, i + 1, S(k), :])

    def speed_y(i, ks):
        for k in ks:
            wy[i, A(k), :] = SCALE * (v[1, i + 1, below(k), :] + v[1, i + 1, S(k), :])

    beside = (3, 4, 13, 14)

    def local_work(g, _):
        winds(g).wait()

        @pl.when(g == 1)
        def _():
            for copy in loads:
                copy.start()

        for h in range(8):
            x = g * 8 + h
            qt[h, OWN, :] = v[2, x + 1, OWN, :].T
            east, north = v[0, x + 1, OWN, :], v[1, x + 1, OWN, :]
            levels = (east * east + north * north).T
            total = profile_weights[0] * levels[0:1]
            for level in range(1, 4):
                total = total + profile_weights[level] * levels[level:level + 1]
            stress[pl.ds(x, 1), :] = total
        for h in range(8):
            x = g * 8 + h
            speed_y(x, [k for k in range(N) if k not in beside])
            if h:
                speed_x(x)
            for k in range(N):
                wz[x, A(k), :] = SCALE * (qt[h, below(k), :] + qt[h, S(k), :])
        return 0

    lax.fori_loop(0, X // 8, local_work, 0)
    for x in range(8, X, 8):
        speed_x(x)

    def column(row):
        spot = lax.broadcasted_iota(jnp.int32, (X, X), 0) == lax.broadcasted_iota(jnp.int32, (X, X), 1)
        return jnp.sum(jnp.where(spot, jnp.broadcast_to(row, (X, X)), 0.0), axis=1, keepdims=True)

    highest = lax.Precision.HIGHEST
    for copy in small:
        copy.wait()
    owner = tile[...].astype(f32)
    same = jnp.broadcast_to(owner, (X, X)) == column(owner)
    sooner = lax.broadcasted_iota(jnp.int32, (X, X), 0) < lax.broadcasted_iota(jnp.int32, (X, X), 1)
    rank = jnp.sum(jnp.where(same & sooner, 1.0, 0.0), axis=0, keepdims=True)
    slot = owner * 2.0 + rank
    placing = jnp.where(
        jnp.broadcast_to(slot, (2 * GX, X))
        == lax.broadcasted_iota(jnp.int32, (2 * GX, X), 0).astype(f32), 1.0, 0.0)
    packed[...] = jnp.dot(placing, stress[...], precision=highest, preferred_element_type=f32)

    def tiles_to(j):
        o = peer(j)
        return pltpu.make_async_remote_copy(
            src_ref=packed.at[pl.ds(2 * o, 2), :], dst_ref=got.at[pl.ds(2 * gx, 2), :],
            send_sem=a2a_sem.at[0], recv_sem=a2a_sem.at[1],
            device_id={"gx": o}, device_id_type=MESH)

    def rows_to(j):
        o = peer(j)
        return pltpu.make_async_remote_copy(
            src_ref=rows.at[pl.ds(o, 1), :], dst_ref=landed.at[pl.ds(gx, 1), :],
            send_sem=a2a_sem.at[2], recv_sem=a2a_sem.at[3],
            device_id={"gx": o}, device_id_type=MESH)

    def send_all(copy):
        def body(j, _):
            copy(j).start()
            return 0
        lax.fori_loop(1, GX, body, 0)

    def wait_all(ref, count, s):
        part = ref.at[pl.ds(0, count), :]
        pltpu.make_async_copy(part, part, a2a_sem.at[s]).wait()

    send_all(tiles_to)
    for c in range(3):
        spin[c].start(along_x)
    wind.start(along_x)
    got[pl.ds(2 * gx, 2), :] = packed[pl.ds(2 * gx, 2), :]

    wind.wait_recv(along_y)

    def speeds_y(g, _):
        for h in range(8):
            speed_y(g * 8 + h, beside)
        return 0

    lax.fori_loop(0, X // 8, speeds_y, 0)

    def parcels():
        wait_all(got, 2 * (GX - 1), 1)
        lifting = jnp.maximum(got[...] - thr[...], 0.0)
        flux = jnp.sum(lifting, axis=0, keepdims=True) / X
        flux_out[...] = flux
        reach = lax.broadcasted_iota(jnp.int32, (X, 128), 1).astype(f32) < column(count[...].astype(f32))
        masses = flux * share[...] * jnp.where(reach, 1.0, 0.0)
        going = jnp.where(
            jnp.broadcast_to(parcel[...], (GX, X)) == lax.broadcasted_iota(jnp.int32, (GX, X), 0), 1.0, 0.0)
        rows[...] = jnp.dot(going, masses, precision=highest, preferred_element_type=f32)
        send_all(rows_to)
        landed[pl.ds(gx, 1), :] = rows[pl.ds(gx, 1), :]

    def deposit():
        wait_all(landed, GX - 1, 3)
        loads[3].wait()
        top = lax.broadcasted_iota(jnp.int32, (128, 128), 0) == 0

        def body(g, _):
            for h in range(8):
                x = g * 8 + h
                drop = jnp.where(top, jnp.broadcast_to(landed[pl.ds(x, 1), :], (128, 128)), 0.0).T
                q[3, x + 2, OWN, :] = q[3, x + 2, OWN, :] + drop
            return 0

        lax.fori_loop(0, X // 8, body, 0)
        dust.start(along_y)
        dust.start(along_x)

    def patch(c):
        def body(x, _):
            q1[c, x + 2, pl.ds(6, 2), :] = yh[0, c, x]
            q1[c, x + 2, pl.ds(136, 2), :] = yh[1, c, x]
            return 0
        lax.fori_loop(0, X, body, 0)

    def keep(c, x, u, value):
        q1[c, x + 2, S(u), :] = value

    def keep_last(c, x, u, value):
        ov[x, S(u), :] = value

    work = (wx, wy, wz, cx, qt, zt, az)
    nothing = lambda j: None

    def edges_come():
        for c in range(3):
            spin[c].wait_recv(along_x)
        wind.wait_recv(along_x)
        speed_x(0)
        speed_x(X)

    def spin_before(j):
        pl.when(j == PARCELS_AT)(parcels)
        pl.when(j == DEPOSIT_AT)(deposit)
        pl.when(j == PAIRS - 2)(edges_come)

    for c in range(3):
        loads[c].wait()
        spin[c].wait_recv(along_y)
    sweep(((0, 1, 2),), q, keep, *work, 1, spin_before, nothing)
    for c in range(3):
        second[c].start(along_y)
        second[c].start(along_x)
    dust.wait_recv(along_y)
    sweep(((3,),), q, keep, *work, 1,
          lambda j: pl.when(j == PAIRS - 2)(lambda: dust.wait_recv(along_x)), nothing)
    second[3].start(along_y)
    second[3].start(along_x)
    second[0].wait_recv(along_y)
    patch(0)
    sweep(((0,),), q1, keep_last, *work, 1,
          lambda j: pl.when(j == PAIRS - 2)(lambda: second[0].wait_recv(along_x)), nothing)
    for c in range(1, 4):
        second[c].wait_recv(along_y)
        patch(c)
        second[c].wait_recv(along_x)

    wait_all(packed, 2 * (GX - 1), 0)
    wait_all(rows, GX - 1, 2)
    for exchange in [wind, dust] + spin + second:
        exchange.wait_send()


def second_kernel(q1, wx, wy, wz, ov0, flux_in, out, flux_out, ov, cx, qt, zt, az, osem):
    ready = pltpu.make_async_copy(ov0.at[:, OWN, :], out.at[0], osem.at[1])
    ready.start()
    flux_out[...] = flux_in[...]
    clear_turned(qt)

    def keep(c, x, u, value):
        ov[c - 1, x, S(u), :] = value

    def out_pair(j):
        pltpu.make_async_copy(
            ov.at[:, pl.ds(2 * j, 2), OWN, :], out.at[pl.ds(1, 3), pl.ds(2 * j, 2)], osem.at[0]).start()

    sweep(((1, 2, 3),), q1, keep, wx, wy, wz, cx, qt, zt, az, 0, lambda j: None, out_pair)
    pltpu.make_async_copy(ov.at[:, :, OWN, :], out.at[pl.ds(1, 3)], osem.at[0]).wait()
    ready.wait()


def shards(state, velocity, threshold, tile_owner, parcel_owner, parcel_count, parcel_share):
    def vm(*shape):
        return pltpu.VMEM(shape, f32)

    def like(*shape):
        return jax.ShapeDtypeStruct(shape, f32)

    hbm = pl.BlockSpec(memory_space=pltpu.HBM)

    def far(x):
        return pltpu.with_memory_space_constraint(x, pltpu.HBM)

    vmem = pl.BlockSpec(memory_space=pltpu.VMEM)
    work = [vm(4, 3, 8 * N, 128)] + [vm(8, ROWS, 128)] * 3
    *between, flux = pl.pallas_call(
        first_kernel,
        out_shape=(vm(4, X + 4, ROWS, 128), vm(X + 1, 8 * N, 128), vm(X, 8 * N, 128),
                   vm(X, 8 * N, 128), vm(X, ROWS, 128), like(1, 128)),
        in_specs=[hbm] * 7,
        out_specs=(vmem,) * 6,
        scratch_shapes=[vm(4, X + 4, ROWS, 128), vm(3, X + 2, ROWS, 128), vm(2, 4, X, 2, 128)]
        + work
        + [vm(X, 128), vm(2 * GX, 128), vm(2 * GX, 128), vm(GX, 128), vm(GX, 128),
           vm(1, 128)] + [pltpu.VMEM((1, X), jnp.int32)] * 3 + [vm(X, 128),
           pltpu.SemaphoreType.DMA((13,)), pltpu.SemaphoreType.DMA((10, 4)), pltpu.SemaphoreType.DMA((10, 4)),
           pltpu.SemaphoreType.DMA((4,))],
        compiler_params=pltpu.CompilerParams(
            collective_id=0, has_side_effects=True, vmem_limit_bytes=24 << 20),
    )(*map(far, (state, velocity, threshold, tile_owner.reshape(1, X), parcel_owner.reshape(1, X),
                 parcel_count, parcel_share.reshape(X, 128))))
    return pl.pallas_call(
        second_kernel,
        out_shape=(like(4, X, 128, 128), like(1, 128)),
        in_specs=[vmem] * 6,
        out_specs=(hbm, vmem),
        scratch_shapes=[vm(3, X, ROWS, 128)] + work + [pltpu.SemaphoreType.DMA((2,))],
        compiler_params=pltpu.CompilerParams(vmem_limit_bytes=16 << 20),
    )(*between, flux)


def solution(mesh):
    return jax.shard_map(
        shards,
        mesh=mesh,
        in_specs=(
            P(None, "gx", "gy", None),
            P(None, "gx", "gy", None),
            P("gx", "gy"),
            P("gy", "gx", None),
            P("gy", "gx", None),
            P("gy", "gx"),
            P("gy", "gx", None),
        ),
        out_specs=(P(None, "gx", "gy", None), P("gx", "gy")),
        check_vma=False,
    )
```
